512 devices in a mesh: row: 32 (over z, y_hi, core), col: 16 (over y_lo, x).
Axes of the slice: x: 4, y: 8 (y_hi: 2, y_lo: 4; y = y_hi * 4 + y_lo), z: 8, core: 2. Of those that a mesh axis runs over, the one named last changes fastest.
Arguments:
- upper: bfloat16 [16384, 32768], P('col', 'row'), may hold values from -6 to 6
- lower: bfloat16 [32768, 16384], P('col', 'row'), may hold values from -0.15625 to 0.15625
- upper_tiles: int32 [128, 256], P('col', 'row'), may hold values from 0 to 1, as said below
- lower_tiles: int32 [256, 128], P('col', 'row'), may hold values from 0 to 1, as said below
Outputs:
- enlarged: bfloat16 [16384, 16384], P('col', 'row')
The draws below stay inside these ranges and needn't reach their ends.
Inputs may be any that keep to these rules, and one draw needn't show every extreme that they name: `upper_tiles`: a tile is 1 exactly where the charge of its row tile equals the charge of its contracted tile (upper) or the charge of its contracted tile equals that of its column tile (lower), charges 0, 1 or 2, laid out in the stored rotated order; both halves share the contracted tiles' charges. `lower_tiles`: charge occupancy of the lower half as described for upper_tiles.
All inputs are finite; a program needn't handle non-finite values.
Results may differ from the reference program's by a relative error of at most 0.001.
Values may be sent and summed in bfloat16 or wider, within the bound.
A program may use at most 64 MiB of HBM per device.

```python
import jax
import jax.numpy as jnp
from jax import lax

K = 32768
TILE = 128
ROWS_DEV = 1024
COLS_DEV = 512
STEPS = 4
ROWS = 16384
COLS = 16384
BLOCK = 1024
RATIO = 2
N_ROW = 32
N_COL = 16


def tile_charges(key):
    first, second, third = jax.random.split(key, 3)
    row_charge = jnp.sum(jax.random.randint(first, (ROWS // TILE, 2), 0, 2), axis=1).astype(jnp.int32)
    inner_charge = jnp.sum(jax.random.randint(second, (K // TILE, 2), 0, 2), axis=1).astype(jnp.int32)
    col_charge = jnp.sum(jax.random.randint(third, (COLS // TILE, 2), 0, 2), axis=1).astype(jnp.int32)
    return (row_charge, inner_charge, col_charge)


def draw_upper_tiles(key, part):
    row_charge, inner_charge, col_charge = tile_charges(key)
    nblocks = K // BLOCK
    per_block = BLOCK // TILE
    row_tiles = jnp.arange(ROWS // TILE, dtype=jnp.int32)
    inner_tiles = jnp.arange(K // TILE, dtype=jnp.int32)
    row_block = row_tiles // (ROWS_DEV // TILE)
    stored_block = inner_tiles // per_block
    offset = inner_tiles % per_block
    logical = (stored_block[None, :] + RATIO * row_block[:, None]) % nblocks * per_block + offset[None, :]
    return (row_charge[:, None] == inner_charge[logical]).astype(jnp.int32)


def draw_lower_tiles(key, part):
    row_charge, inner_charge, col_charge = tile_charges(key)
    nblocks = K // BLOCK
    per_block = BLOCK // TILE
    inner_tiles = jnp.arange(K // TILE, dtype=jnp.int32)
    col_tiles = jnp.arange(COLS // TILE, dtype=jnp.int32)
    col_block = col_tiles // (COLS_DEV // TILE)
    stored_block = inner_tiles // per_block
    offset = inner_tiles % per_block
    logical = (stored_block[:, None] + col_block[None, :]) % nblocks * per_block + offset[:, None]
    return (inner_charge[logical] == col_charge[None, :]).astype(jnp.int32)


def steps_of(rng, shape, pieces, least, top_value):
    factor_of, own = 1.0, jax.random.fold_in(rng, 6)
    for position, parts in pieces:
        steps = jnp.exp(jax.random.uniform(jax.random.fold_in(own, position), (parts,), jnp.float32, least / len(pieces), top_value / len(pieces)))
        factor_of = factor_of * jnp.repeat(steps, shape[position] // parts).reshape([-1 if axis == position else 1 for axis in range(len(shape))])
    return factor_of


def gaussian(key, extent, scale, limit, pieces=(), kind=jnp.bfloat16):
    values = jax.random.normal(key, extent, jnp.float32) * scale
    if len(pieces) > 0:
        values = steps_of(key, extent, pieces, -0.22, 0.18) * values
    return jnp.clip(values, min=-limit, max=limit).astype(kind)


def setup_inputs(seed: int = 0) -> dict:
    key_list = jax.random.split(jax.random.key(seed), 5)
    upper = gaussian(key_list[0], (ROWS, K), 1.0, 6.0, ((0, 16), (1, 32)))
    lower = gaussian(key_list[1], (K, COLS), (STEPS * BLOCK * 3 // 8) ** -0.5, 0.15625, ((0, 16), (1, 32)))
    upper_tiles = draw_upper_tiles(jax.random.fold_in(key_list[4], 71), 0)
    lower_tiles = draw_lower_tiles(jax.random.fold_in(key_list[4], 71), 0)
    return {"upper": upper, "lower": lower, "upper_tiles": upper_tiles, "lower_tiles": lower_tiles}


def apply_tiles(values, tiles, tile_size):
    rows, cols = values.shape
    shaped = values.reshape(rows // tile_size, tile_size, cols // tile_size, tile_size)
    masked = shaped * tiles.astype(values.dtype)[:, None, :, None]
    return masked.reshape(rows, cols)


def reference(upper, lower, upper_tiles, lower_tiles):
    tile_size = K // upper_tiles.shape[1]
    masked_upper = apply_tiles(upper, upper_tiles, tile_size)
    masked_lower = apply_tiles(lower, lower_tiles, tile_size)
    block = K // N_ROW
    ratio = N_ROW // N_COL
    rows_dev = upper.shape[0] // N_COL
    cols_dev = lower.shape[1] // N_ROW
    upper_blocks = masked_upper.reshape(N_COL, rows_dev, N_ROW, block)
    lower_blocks = masked_lower.reshape(N_ROW, block, N_ROW, cols_dev)
    col_range = jnp.arange(N_ROW, dtype=jnp.int32)

    def one_rowblock(row_block):
        mine = upper_blocks[row_block]
        result = jnp.zeros((N_ROW, rows_dev, cols_dev), jnp.float32)
        for step_index in range(STEPS):
            picks = ((col_range + step_index) % N_ROW).astype(jnp.int32)
            chosen = jnp.take(mine, picks, axis=1).astype(jnp.float32)
            lower_index = ((ratio * row_block + step_index) % N_ROW).astype(jnp.int32)
            lower_rows = jnp.take(lower_blocks, lower_index, axis=0).astype(jnp.float32)
            result = result + jnp.einsum("mrk,krn->rmn", chosen, lower_rows, precision=lax.Precision.HIGHEST)
        return result

    outputs = lax.map(one_rowblock, jnp.arange(N_COL, dtype=jnp.int32))
    enlarged = jnp.transpose(outputs, (0, 2, 1, 3)).reshape(N_COL * rows_dev, N_ROW * cols_dev)
    return enlarged.astype(jnp.bfloat16)
```

```python
import jax
import jax.numpy as jnp
from jax import lax
from jax.experimental import pallas as pl
from jax.experimental.pallas import tpu as pltpu
from jax.sharding import PartitionSpec as P

STEPS = 4
TILE = 128
X = 4
PARTS = 4
MESH = pl.DeviceIdType.MESH


def kernel(
    n_row, n_col, upper_tiles, lower_tiles, upper, lower, out,
    ublocks, lblocks, relay, result,
    uload, lload, near_send, near_recv, far_send, far_recv, pair_send, pair_recv,
    low_send, low_recv, hop_send, hop_recv, store_sem,
):
    r, c = lax.axis_index("row"), lax.axis_index("col")
    core, x = r % 2, c % X
    even = core == 0
    rows = TILE
    chunks = upper.shape[0] // rows
    held = lower.shape[0]
    quarter = held // PARTS

    def dev(dr, dc):
        return (lax.rem(r + dr + n_row, n_row), lax.rem(c + dc + n_col, n_col))

    first = x == 0
    last = x == X - 1
    origin_c = c - x
    goal = (r, lax.rem(origin_c + n_col - 1, n_col))

    barrier = pltpu.get_barrier_semaphore()

    def greet(device):
        pl.semaphore_signal(barrier, inc=1, device_id=device, device_id_type=MESH)

    for i in range(chunks):
        pltpu.make_async_copy(
            upper.at[pl.ds(i * rows, rows)], ublocks.at[0, pl.ds(i * rows, rows)], uload.at[i]
        ).start()
    for i in range(PARTS):
        pltpu.make_async_copy(
            lower.at[pl.ds(i * quarter, quarter)], lblocks.at[pl.ds(i * quarter, quarter)], lload.at[i]
        ).start()

    greet(dev(2, 0))
    greet(dev(jnp.where(even, 1, 3), 0))
    greet(dev(jnp.where(even, 1, -1), 0))

    @pl.when(jnp.logical_not(last))
    def _():
        greet(dev(0, 1))

    @pl.when(last)
    def _():
        for j in range(PARTS):
            greet((r, lax.rem(origin_c + X + j, n_col)))

    @pl.when(jnp.logical_not(first))
    def _():
        greet((r, origin_c))

    pl.semaphore_wait(barrier, jnp.where(first, 3 + 1 + 3, 3 + 1 + 1))

    def near(i):
        part = pl.ds(pl.multiple_of(i * rows, rows), rows)
        return pltpu.make_async_remote_copy(
            ublocks.at[0, part], ublocks.at[2, part], near_send.at[i], near_recv.at[i],
            device_id=dev(-2, 0), device_id_type=MESH,
        )

    def far(i):
        part = pl.ds(pl.multiple_of(i * rows, rows), rows)
        return pltpu.make_async_remote_copy(
            ublocks.at[0, part], ublocks.at[jnp.where(even, 3, 1), part], far_send.at[i], far_recv.at[i],
            device_id=dev(jnp.where(even, -3, -1), 0), device_id_type=MESH,
        )

    def pair(i):
        part = pl.ds(pl.multiple_of(i * rows, rows), rows)
        return pltpu.make_async_remote_copy(
            ublocks.at[2, part], ublocks.at[jnp.where(even, 1, 3), part], pair_send.at[i], pair_recv.at[i],
            device_id=dev(jnp.where(even, 1, -1), 0), device_id_type=MESH,
        )

    def low(j):
        return pltpu.make_async_remote_copy(
            lblocks.at[pl.ds(j * quarter, quarter)], lblocks.at[pl.ds(held + j * quarter, quarter)],
            low_send.at[j], low_recv.at[j], device_id=dev(0, -1), device_id_type=MESH,
        )

    def hop(j):
        return pltpu.make_async_remote_copy(
            lblocks.at[pl.ds(j * quarter, quarter)], relay, hop_send.at[j], hop_recv.at[0],
            device_id=(r, lax.rem(origin_c + j, n_col)), device_id_type=MESH,
        )

    def goal_first():
        return pltpu.make_async_remote_copy(
            lblocks.at[pl.ds(0, quarter)], lblocks.at[pl.ds(held, quarter)],
            low_send.at[0], low_recv.at[0], device_id=goal, device_id_type=MESH,
        )

    def goal_relay():
        return pltpu.make_async_remote_copy(
            relay, lblocks.at[pl.ds(pl.multiple_of(held + x * quarter, quarter), quarter)],
            hop_send.at[0], low_recv.at[x], device_id=goal, device_id_type=MESH,
        )

    def mask_upper(i):
        part = pl.ds(pl.multiple_of(i * rows, rows), rows)
        for k in range(upper.shape[1] // TILE):
            at = (0, part, pl.ds(k * TILE, TILE))
            keep = upper_tiles[i, k].astype(jnp.float32)
            ublocks[at] = ublocks[at] * jnp.full((rows, TILE), keep, jnp.float32).astype(jnp.bfloat16)

    def mask_lower(i):
        part = pl.ds(pl.multiple_of(i * TILE, TILE), TILE)
        for k in range(lower.shape[1] // TILE):
            at = (part, pl.ds(k * TILE, TILE))
            keep = lower_tiles[i, k].astype(jnp.float32)
            lblocks[at] = lblocks[at] * jnp.full((TILE, TILE), keep, jnp.float32).astype(jnp.bfloat16)

    @pl.loop(0, chunks)
    def _(i):
        part = pl.ds(pl.multiple_of(i * rows, rows), rows)
        pltpu.make_async_copy(upper.at[part], ublocks.at[0, part], uload.at[i]).wait()
        mask_upper(i)
        near(i).start()
        far(i).start()

    for i in range(PARTS):
        pltpu.make_async_copy(
            lower.at[pl.ds(i * quarter, quarter)], lblocks.at[pl.ds(i * quarter, quarter)], lload.at[i]
        ).wait()

    @pl.loop(0, held // TILE)
    def _(i):
        mask_lower(i)

    @pl.when(first)
    def _():
        for j in range(1, PARTS):
            hop(j).start()
        goal_first().start()

    @pl.when(jnp.logical_not(first))
    def _():
        for j in range(PARTS):
            low(j).start()
        hop(1).wait_recv()
        goal_relay().start()

    def multiply(i):
        part = pl.ds(pl.multiple_of(i * rows, rows), rows)
        block = ublocks.shape[2]
        total = jnp.zeros((rows, lower.shape[1]), jnp.float32)
        for s in range(STEPS):
            total += jnp.dot(
                ublocks[s, part], lblocks[pl.ds(s * block, block)], preferred_element_type=jnp.float32
            )
        result[part] = total.astype(jnp.bfloat16)
        pltpu.make_async_copy(result.at[part], out.at[part], store_sem.at[i]).start()

    near(0).wait_recv()
    pair(0).start()
    for j in range(PARTS):
        low(j).wait_recv()

    @pl.loop(1, chunks)
    def _(i):
        near(i).wait_recv()
        pair(i).start()
        pair(i - 1).wait_recv()
        far(i - 1).wait_recv()
        multiply(i - 1)

    pair(chunks - 1).wait_recv()
    far(chunks - 1).wait_recv()
    multiply(chunks - 1)

    @pl.loop(0, chunks)
    def _(i):
        part = pl.ds(pl.multiple_of(i * rows, rows), rows)
        near(i).wait_send()
        far(i).wait_send()
        pair(i).wait_send()
        pltpu.make_async_copy(result.at[part], out.at[part], store_sem.at[i]).wait()

    @pl.when(first)
    def _():
        for j in range(1, PARTS):
            hop(j).wait_send()
        goal_first().wait_send()

    @pl.when(jnp.logical_not(first))
    def _():
        for j in range(PARTS):
            low(j).wait_send()
        goal_relay().wait_send()


def body(upper, lower, upper_tiles, lower_tiles):
    n_row, n_col = lax.axis_size("row"), lax.axis_size("col")
    rows, block = upper.shape
    held, cols = lower.shape
    chunks = rows // TILE
    dma = pltpu.SemaphoreType.DMA

    def run(*refs):
        kernel(n_row, n_col, *refs)

    return pl.pallas_call(
        run,
        out_shape=jax.ShapeDtypeStruct((rows, cols), jnp.bfloat16),
        in_specs=[pl.BlockSpec(memory_space=pltpu.SMEM)] * 2 + [pl.BlockSpec(memory_space=pl.ANY)] * 2,
        out_specs=pl.BlockSpec(memory_space=pl.ANY),
        scratch_shapes=[
            pltpu.VMEM((STEPS, rows, block), jnp.bfloat16),
            pltpu.VMEM((2 * held, cols), jnp.bfloat16),
            pltpu.VMEM((held // PARTS, cols), jnp.bfloat16),
            pltpu.VMEM((rows, cols), jnp.bfloat16),
            dma((chunks,)), dma((PARTS,)),
            dma((chunks,)), dma((chunks,)),
            dma((chunks,)), dma((chunks,)),
            dma((chunks,)), dma((chunks,)),
            dma((PARTS,)), dma((PARTS,)),
            dma((PARTS,)), dma((1,)),
            dma((chunks,)),
        ],
        compiler_params=pltpu.CompilerParams(
            collective_id=0, has_side_effects=True, vmem_limit_bytes=40 * 1024 * 1024
        ),
        cost_estimate=pl.CostEstimate(
            flops=2 * STEPS * rows * block * cols,
            bytes_accessed=2 * (rows * block + held * cols + rows * cols),
            transcendentals=0,
        ),
        name="corner_product",
    )(upper_tiles, lower_tiles, upper, lower)


def solution(mesh):
    spec = P("col", "row")
    return jax.shard_map(body, mesh=mesh, in_specs=(spec,) * 4, out_specs=spec, check_vma=False)
```

```python
import jax
import jax.numpy as jnp
from jax import lax
from jax.experimental import pallas as pl
from jax.experimental.pallas import tpu as pltpu
from jax.sharding import PartitionSpec as P

STEPS = 4
TILE = 128
X = 4
SUB = 1
BEGIN = 3
LATE = 3
PIECES = 4
ORDER = (1, 2, 3, 0)
PARTS = 4
MESH = pl.DeviceIdType.MESH


def kernel(
    n_row, n_col, upper_tiles_in, lower_tiles_in, upper, lower, out,
    upper_tiles, lower_tiles, tile_load, ublocks, lblocks, relay,
    uload, lload, near_send, near_recv, far_send, far_recv, pair_send, pair_recv,
    low_send, low_recv, hop_send, hop_recv, goal_recv,
):
    r, c = lax.axis_index("row"), lax.axis_index("col")
    core, x = r % 2, c % X
    even = core == 0
    rows = TILE
    chunks = upper.shape[0] // rows
    held = lower.shape[0]
    quarter = held // PARTS

    def dev(dr, dc):
        return (lax.rem(r + dr + n_row, n_row), lax.rem(c + dc + n_col, n_col))

    first = x == 0
    last = x == X - 1
    origin_c = c - x
    goal = (r, lax.rem(origin_c + n_col - 1, n_col))

    barrier = pltpu.get_barrier_semaphore()

    def greet(device):
        pl.semaphore_signal(barrier, inc=1, device_id=device, device_id_type=MESH)

    tile_loads = (
        pltpu.make_async_copy(lower_tiles_in, lower_tiles, tile_load.at[0]),
        pltpu.make_async_copy(upper_tiles_in, upper_tiles, tile_load.at[1]),
    )
    for load in tile_loads:
        load.start()
    def load_upper(i):
        part = pl.ds(pl.multiple_of(i * rows, rows), rows)
        return pltpu.make_async_copy(upper.at[part], ublocks.at[0, part], uload.at[i])

    def load_lower(j):
        part = pl.ds(j * quarter, quarter)
        return pltpu.make_async_copy(lower.at[part], lblocks.at[part], lload.at[j])

    for i in range(BEGIN):
        load_upper(i).start()
    for j in ORDER:
        load_lower(j).start()
    for i in range(BEGIN, chunks):
        load_upper(i).start()

    greet(dev(2, 0))
    greet(dev(jnp.where(even, 1, 3), 0))
    greet(dev(jnp.where(even, 1, -1), 0))

    @pl.when(jnp.logical_not(last))
    def _():
        greet(dev(0, 1))

    @pl.when(last)
    def _():
        for j in range(PARTS):
            greet((r, lax.rem(origin_c + X + j, n_col)))

    @pl.when(jnp.logical_not(first))
    def _():
        greet((r, origin_c))

    pl.semaphore_wait(barrier, jnp.where(first, 3 + 1 + 3, 3 + 1 + 1))

    fine = rows // SUB
    nears = chunks * SUB

    def near(i):
        part = pl.ds(pl.multiple_of(i * fine, fine), fine)
        return pltpu.make_async_remote_copy(
            ublocks.at[0, part], ublocks.at[2, part], near_send.at[i], near_recv.at[i],
            device_id=dev(-2, 0), device_id_type=MESH,
        )

    def far(i):
        part = pl.ds(pl.multiple_of(i * rows, rows), rows)
        return pltpu.make_async_remote_copy(
            ublocks.at[0, part], ublocks.at[jnp.where(even, 3, 1), part], far_send.at[i], far_recv.at[i],
            device_id=dev(jnp.where(even, -3, -1), 0), device_id_type=MESH,
        )

    def pair(i):
        part = pl.ds(pl.multiple_of(i * fine, fine), fine)
        return pltpu.make_async_remote_copy(
            ublocks.at[2, part], ublocks.at[jnp.where(even, 1, 3), part], pair_send.at[i], pair_recv.at[i],
            device_id=dev(jnp.where(even, 1, -1), 0), device_id_type=MESH,
        )

    def low(j):
        return pltpu.make_async_remote_copy(
            lblocks.at[pl.ds(j * quarter, quarter)], lblocks.at[pl.ds(held + j * quarter, quarter)],
            low_send.at[j], low_recv.at[j], device_id=dev(0, -1), device_id_type=MESH,
        )

    piece = quarter // PIECES

    def hop(j, h):
        return pltpu.make_async_remote_copy(
            lblocks.at[pl.ds(j * quarter + h * piece, piece)], relay.at[pl.ds(h * piece, piece)],
            hop_send.at[j, h], hop_recv.at[h],
            device_id=(r, lax.rem(origin_c + j, n_col)), device_id_type=MESH,
        )

    def goal_first(h):
        return pltpu.make_async_remote_copy(
            lblocks.at[pl.ds(h * piece, piece)], lblocks.at[pl.ds(held + h * piece, piece)],
            hop_send.at[0, h], goal_recv.at[0, h], device_id=goal, device_id_type=MESH,
        )

    def goal_relay(h):
        return pltpu.make_async_remote_copy(
            relay.at[pl.ds(h * piece, piece)],
            lblocks.at[pl.ds(pl.multiple_of(held + x * quarter + h * piece, piece), piece)],
            hop_send.at[0, h], goal_recv.at[x, h], device_id=goal, device_id_type=MESH,
        )

    def goal_wait(j, h):
        return pltpu.make_async_remote_copy(
            relay.at[pl.ds(h * piece, piece)],
            lblocks.at[pl.ds(held + j * quarter + h * piece, piece)],
            hop_send.at[0, h], goal_recv.at[j, h], device_id=goal, device_id_type=MESH,
        )

    def mask_upper(i):
        part = pl.ds(pl.multiple_of(i * rows, rows), rows)
        for k in range(upper.shape[1] // TILE):
            at = (0, part, pl.ds(k * TILE, TILE))
            keep = upper_tiles[i, k].astype(jnp.float32)
            ublocks[at] = ublocks[at] * jnp.full((rows, TILE), keep, jnp.float32).astype(jnp.bfloat16)

    def mask_lower(i):
        part = pl.ds(pl.multiple_of(i * TILE, TILE), TILE)
        for k in range(lower.shape[1] // TILE):
            at = (part, pl.ds(k * TILE, TILE))
            keep = lower_tiles[k, i].astype(jnp.float32)
            lblocks[at] = lblocks[at] * jnp.full((TILE, TILE), keep, jnp.float32).astype(jnp.bfloat16)

    for load in tile_loads:
        load.wait()

    def begin_near():
        @pl.loop(0, BEGIN)
        def _(i):
            load_upper(i).wait()
            mask_upper(i)
            for n in range(SUB):
                near(i * SUB + n).start()

    @pl.when(jnp.logical_not(first))
    def _():
        begin_near()

    for j in ORDER:
        load_lower(j).wait()

        @pl.loop(0, quarter // TILE)
        def _(h):
            mask_lower(j * (quarter // TILE) + h)

        @pl.when(first)
        def _():
            for h in range(PIECES):
                if j == 0:
                    goal_first(h).start()
                else:
                    hop(j, h).start()

    @pl.when(first)
    def _():
        begin_near()

    @pl.loop(0, BEGIN)
    def _(i):
        far(i).start()

    @pl.loop(BEGIN, chunks)
    def _(i):
        load_upper(i).wait()
        mask_upper(i)
        far(i).start()

    @pl.when(jnp.logical_not(first))
    def _():
        for h in range(PIECES):
            hop(1, h).wait_recv()
            goal_relay(h).start()
        for j in range(PARTS):
            low(j).start()

    @pl.loop(BEGIN * SUB, nears)
    def _(i):
        near(i).start()

    def multiply(i):
        part = pl.ds(pl.multiple_of(i * rows, rows), rows)
        block = ublocks.shape[2]
        total = jnp.zeros((rows, lower.shape[1]), jnp.float32)
        for s in range(STEPS):
            total += jnp.dot(
                ublocks[s, part], lblocks[pl.ds(s * block, block)], preferred_element_type=jnp.float32
            )
        out[part] = total.astype(jnp.bfloat16)

    def step(i):
        near(i).wait_recv()
        pair(i).start()

    def finish(i):
        for n in range(SUB):
            pair(i * SUB + n).wait_recv()
        far(i).wait_recv()
        multiply(i)

    late = nears - LATE

    @pl.loop(0, late)
    def _(i):
        step(i)

    @pl.when(jnp.logical_not(last))
    def _():
        for j in range(PARTS):
            low(j).wait_recv()

    @pl.when(last)
    def _():
        for j in range(PARTS):
            for h in range(PIECES):
                goal_wait(j, h).wait_recv()

    @pl.loop(late, nears)
    def _(i):
        step(i)

        @pl.loop((i - late) * (chunks - 1) // LATE, (i + 1 - late) * (chunks - 1) // LATE)
        def _(n):
            finish(n)

    finish(chunks - 1)

    @pl.loop(0, nears)
    def _(i):
        near(i).wait_send()
        pair(i).wait_send()

    @pl.loop(0, chunks)
    def _(i):
        far(i).wait_send()

    @pl.when(first)
    def _():
        for h in range(PIECES):
            for j in range(1, PARTS):
                hop(j, h).wait_send()
            goal_first(h).wait_send()

    @pl.when(jnp.logical_not(first))
    def _():
        for j in range(PARTS):
            low(j).wait_send()
        for h in range(PIECES):
            goal_relay(h).wait_send()


def body(upper, lower, upper_tiles, lower_tiles):
    n_row, n_col = lax.axis_size("row"), lax.axis_size("col")
    rows, block = upper.shape
    held, cols = lower.shape
    chunks = rows // TILE
    dma = pltpu.SemaphoreType.DMA

    def run(*refs):
        kernel(n_row, n_col, *refs)

    return pl.pallas_call(
        run,
        out_shape=pltpu.VMEM((rows, cols), jnp.bfloat16),
        in_specs=[pl.BlockSpec(memory_space=pltpu.HBM)] * 4,
        out_specs=pl.BlockSpec(memory_space=pltpu.VMEM),
        scratch_shapes=[
            pltpu.SMEM(upper_tiles.shape, jnp.int32),
            pltpu.SMEM(lower_tiles.shape[::-1], jnp.int32),
            dma((2,)),
            pltpu.VMEM((STEPS, rows, block), jnp.bfloat16),
            pltpu.VMEM((2 * held, cols), jnp.bfloat16),
            pltpu.VMEM((held // PARTS, cols), jnp.bfloat16),
            dma((chunks,)), dma((PARTS,)),
            dma((chunks * SUB,)), dma((chunks * SUB,)),
            dma((chunks,)), dma((chunks,)),
            dma((chunks * SUB,)), dma((chunks * SUB,)),
            dma((PARTS,)), dma((PARTS,)),
            dma((PARTS, PIECES)), dma((PIECES,)), dma((PARTS, PIECES)),
        ],
        compiler_params=pltpu.CompilerParams(
            collective_id=0, has_side_effects=True, vmem_limit_bytes=40 * 1024 * 1024
        ),
        cost_estimate=pl.CostEstimate(
            flops=2 * STEPS * rows * block * cols,
            bytes_accessed=2 * (rows * block + held * cols + rows * cols),
            transcendentals=0,
        ),
        name="corner_product",
    )(*(pltpu.with_memory_space_constraint(a, pltpu.HBM) for a in (upper_tiles, lower_tiles.T, upper, lower)))


def solution(mesh):
    spec = P("col", "row")
    return jax.shard_map(body, mesh=mesh, in_specs=(spec,) * 4, out_specs=spec, check_vma=False)
```

```python
import jax
import jax.numpy as jnp
from jax import lax
from jax.experimental import pallas as pl
from jax.experimental.pallas import tpu as pltpu
from jax.sharding import PartitionSpec as P

STEPS = 4
TILE = 128
X = 4
BEGIN = 3
LATE = 3
PIECES = 4
ORDER = (1, 2, 3, 0)
PARTS = 4
MESH = pl.DeviceIdType.MESH


def kernel(
    n_row, n_col, upper_tiles_in, lower_tiles_in, upper, lower, out,
    upper_tiles, lower_tiles, tile_load, ublocks, lblocks, relay, passed,
    uload, lload, near_send, near_recv, far_send, far_recv, pair_send, pair_recv,
    low_send, low_recv, hop_send, hop_recv, pass_recv, goal_send, goal_recv,
):
    r, c = lax.axis_index("row"), lax.axis_index("col")
    core, x = r % 2, c % X
    even = core == 0
    rows = TILE
    chunks = upper.shape[0] // rows
    held = lower.shape[0]
    quarter = held // PARTS

    def dev(dr, dc):
        return (lax.rem(r + dr + n_row, n_row), lax.rem(c + dc + n_col, n_col))

    first = x == 0
    last = x == X - 1
    origin_c = c - x
    goal = (r, origin_c + X - 1)

    barrier = pltpu.get_barrier_semaphore()

    def greet(device):
        pl.semaphore_signal(barrier, inc=1, device_id=device, device_id_type=MESH)

    greet(dev(2, 0))
    greet(dev(jnp.where(even, 1, 3), 0))
    greet(dev(jnp.where(even, 1, -1), 0))

    @pl.when(jnp.logical_not(last))
    def _():
        greet(dev(0, 1))

    @pl.when(last)
    def _():
        for j in range(PARTS - 1):
            greet((r, origin_c + j))

    greet(dev(0, X))

    @pl.when(jnp.logical_not(first))
    def _():
        greet((r, origin_c))

    tile_loads = (
        pltpu.make_async_copy(lower_tiles_in, lower_tiles, tile_load.at[0]),
        pltpu.make_async_copy(upper_tiles_in, upper_tiles, tile_load.at[1]),
    )
    for load in tile_loads:
        load.start()
    def load_upper(i):
        part = pl.ds(pl.multiple_of(i * rows, rows), rows)
        return pltpu.make_async_copy(upper.at[part], ublocks.at[0, part], uload.at[i])

    def load_lower(j):
        part = pl.ds(j * quarter, quarter)
        return pltpu.make_async_copy(lower.at[part], lblocks.at[part], lload.at[j])

    for i in range(BEGIN):
        load_upper(i).start()
    for j in ORDER:
        load_lower(j).start()
    for i in range(BEGIN, chunks):
        load_upper(i).start()

    def near(i):
        part = pl.ds(pl.multiple_of(i * rows, rows), rows)
        return pltpu.make_async_remote_copy(
            ublocks.at[0, part], ublocks.at[2, part], near_send.at[i], near_recv.at[i],
            device_id=dev(-2, 0), device_id_type=MESH,
        )

    def far(i):
        part = pl.ds(pl.multiple_of(i * rows, rows), rows)
        return pltpu.make_async_remote_copy(
            ublocks.at[0, part], ublocks.at[jnp.where(even, 3, 1), part], far_send.at[i], far_recv.at[i],
            device_id=dev(jnp.where(even, -3, -1), 0), device_id_type=MESH,
        )

    def pair(i):
        part = pl.ds(pl.multiple_of(i * rows, rows), rows)
        return pltpu.make_async_remote_copy(
            ublocks.at[2, part], ublocks.at[jnp.where(even, 1, 3), part], pair_send.at[i], pair_recv.at[i],
            device_id=dev(jnp.where(even, 1, -1), 0), device_id_type=MESH,
        )

    def low(j):
        return pltpu.make_async_remote_copy(
            lblocks.at[pl.ds(j * quarter, quarter)], lblocks.at[pl.ds(held + j * quarter, quarter)],
            low_send.at[j], low_recv.at[j], device_id=dev(0, -1), device_id_type=MESH,
        )

    piece = quarter // PIECES

    def hop(j, h):
        return pltpu.make_async_remote_copy(
            lblocks.at[pl.ds(j * quarter + h * piece, piece)], relay.at[pl.ds(h * piece, piece)],
            hop_send.at[j, h], hop_recv.at[h],
            device_id=(r, lax.rem(origin_c + j, n_col)), device_id_type=MESH,
        )

    def passing(source, target, sem, h):
        return pltpu.make_async_remote_copy(
            source.at[pl.ds(h * piece, piece)], target.at[pl.ds(h * piece, piece)],
            hop_send.at[0, h], sem.at[h], device_id=dev(0, -X), device_id_type=MESH,
        )

    def arrived(j):
        return lblocks.at[pl.ds(pl.multiple_of(held + j * quarter, quarter), quarter)]

    def pass_on(h):
        @pl.when(first)
        def _():
            passing(lblocks.at[pl.ds(0, quarter)], passed, pass_recv, h).start()

        @pl.when(jnp.logical_not(jnp.logical_or(first, last)))
        def _():
            passing(relay, passed, pass_recv, h).start()

        @pl.when(last)
        def _():
            passing(relay, arrived(PARTS - 1), goal_recv.at[PARTS - 1], h).start()

    def to_goal(j, h):
        return pltpu.make_async_remote_copy(
            passed.at[pl.ds(h * piece, piece)], arrived(j).at[pl.ds(h * piece, piece)],
            goal_send.at[h], goal_recv.at[j, h], device_id=goal, device_id_type=MESH,
        )

    def mask_upper(i):
        part = pl.ds(pl.multiple_of(i * rows, rows), rows)
        for k in range(upper.shape[1] // TILE):
            at = (0, part, pl.ds(k * TILE, TILE))
            keep = upper_tiles[i, k].astype(jnp.float32)
            ublocks[at] = ublocks[at] * jnp.full((rows, TILE), keep, jnp.float32).astype(jnp.bfloat16)

    def mask_lower(i):
        part = pl.ds(pl.multiple_of(i * TILE, TILE), TILE)
        for k in range(lower.shape[1] // TILE):
            at = (part, pl.ds(k * TILE, TILE))
            keep = lower_tiles[k, i].astype(jnp.float32)
            lblocks[at] = lblocks[at] * jnp.full((TILE, TILE), keep, jnp.float32).astype(jnp.bfloat16)

    for load in tile_loads:
        load.wait()

    @pl.loop(0, BEGIN)
    def _(i):
        load_upper(i).wait()
        mask_upper(i)

    for j in ORDER:
        load_lower(j).wait()

        @pl.loop(0, quarter // TILE)
        def _(h):
            mask_lower(j * (quarter // TILE) + h)

    pl.semaphore_wait(barrier, 4 + jnp.where(first, 3, 1) + jnp.where(last, 0, 1))

    @pl.loop(0, BEGIN)
    def _(i):
        near(i).start()

    @pl.when(first)
    def _():
        for j in range(1, PARTS):
            for h in range(PIECES):
                hop(j, h).start()

    @pl.when(jnp.logical_not(first))
    def _():
        for j in range(PARTS):
            low(j).start()

    @pl.loop(0, BEGIN)
    def _(i):
        far(i).start()

    @pl.loop(BEGIN, chunks)
    def _(i):
        load_upper(i).wait()
        mask_upper(i)
        far(i).start()

    for h in range(PIECES):
        @pl.when(jnp.logical_not(first))
        def _():
            hop(1, h).wait_recv()

        pass_on(h)

    @pl.loop(BEGIN, chunks)
    def _(i):
        near(i).start()

    @pl.when(jnp.logical_not(last))
    def _():
        for h in range(PIECES):
            passing(relay, passed, pass_recv, h).wait_recv()
            to_goal(x, h).start()

    def multiply(i):
        part = pl.ds(pl.multiple_of(i * rows, rows), rows)
        block = ublocks.shape[2]
        total = jnp.zeros((rows, lower.shape[1]), jnp.float32)
        for s in range(STEPS):
            total += jnp.dot(
                ublocks[s, part], lblocks[pl.ds(s * block, block)], preferred_element_type=jnp.float32
            )
        out[part] = total.astype(jnp.bfloat16)

    def step(i):
        near(i).wait_recv()
        pair(i).start()

    def finish(i):
        pair(i).wait_recv()
        far(i).wait_recv()
        multiply(i)

    late = chunks - LATE

    @pl.loop(0, late)
    def _(i):
        step(i)

    @pl.when(jnp.logical_not(last))
    def _():
        for j in range(PARTS):
            low(j).wait_recv()

    @pl.when(last)
    def _():
        for j in range(PARTS):
            for h in range(PIECES):
                to_goal(j, h).wait_recv()

    @pl.loop(0, late - 1)
    def _(i):
        finish(i)

    @pl.loop(late, chunks)
    def _(i):
        finish(i - 1)
        step(i)

    @pl.loop(0, chunks - 1)
    def _(i):
        near(i).wait_send()
        pair(i).wait_send()
        far(i).wait_send()

    far(chunks - 1).wait_send()

    @pl.when(first)
    def _():
        for h in range(PIECES):
            for j in range(1, PARTS):
                hop(j, h).wait_send()

    @pl.when(jnp.logical_not(first))
    def _():
        for j in range(PARTS):
            low(j).wait_send()

    for h in range(PIECES):
        passing(relay, passed, pass_recv, h).wait_send()

    @pl.when(jnp.logical_not(last))
    def _():
        for h in range(PIECES):
            to_goal(x, h).wait_send()

    finish(chunks - 1)
    near(chunks - 1).wait_send()
    pair(chunks - 1).wait_send()


def body(upper, lower, upper_tiles, lower_tiles):
    n_row, n_col = lax.axis_size("row"), lax.axis_size("col")
    rows, block = upper.shape
    held, cols = lower.shape
    chunks = rows // TILE
    dma = pltpu.SemaphoreType.DMA

    def run(*refs):
        kernel(n_row, n_col, *refs)

    return pl.pallas_call(
        run,
        out_shape=pltpu.VMEM((rows, cols), jnp.bfloat16),
        in_specs=[pl.BlockSpec(memory_space=pltpu.HBM)] * 4,
        out_specs=pl.BlockSpec(memory_space=pltpu.VMEM),
        scratch_shapes=[
            pltpu.SMEM(upper_tiles.shape, jnp.int32),
            pltpu.SMEM(lower_tiles.shape[::-1], jnp.int32),
            dma((2,)),
            pltpu.VMEM((STEPS, rows, block), jnp.bfloat16),
            pltpu.VMEM((2 * held, cols), jnp.bfloat16),
            pltpu.VMEM((held // PARTS, cols), jnp.bfloat16),
            pltpu.VMEM((held // PARTS, cols), jnp.bfloat16),
            dma((chunks,)), dma((PARTS,)),
            dma((chunks,)), dma((chunks,)),
            dma((chunks,)), dma((chunks,)),
            dma((chunks,)), dma((chunks,)),
            dma((PARTS,)), dma((PARTS,)),
            dma((PARTS, PIECES)), dma((PIECES,)), dma((PIECES,)), dma((PIECES,)), dma((PARTS, PIECES)),
        ],
        compiler_params=pltpu.CompilerParams(
            collective_id=0, has_side_effects=True, vmem_limit_bytes=40 * 1024 * 1024
        ),
        cost_estimate=pl.CostEstimate(
            flops=2 * STEPS * rows * block * cols,
            bytes_accessed=2 * (rows * block + held * cols + rows * cols),
            transcendentals=0,
        ),
        name="corner_product",
    )(*(pltpu.with_memory_space_constraint(a, pltpu.HBM) for a in (upper_tiles, lower_tiles.T, upper, lower)))


def solution(mesh):
    spec = P("col", "row")
    return jax.shard_map(body, mesh=mesh, in_specs=(spec,) * 4, out_specs=spec, check_vma=False)
```

```python
import jax
import jax.numpy as jnp
from jax import lax
from jax.experimental import pallas as pl
from jax.experimental.pallas import tpu as pltpu
from jax.sharding import PartitionSpec as P

STEPS = 4
TILE = 128
X = 4
BEGIN = 3
LATE = 3
FARS = 2
PIECES = 1
ORDER = (1, 2, 3, 0)
PARTS = 4
MESH = pl.DeviceIdType.MESH


def kernel(
    n_row, n_col, upper_tiles_in, lower_tiles_in, upper, lower, out,
    upper_tiles, lower_tiles, tile_load, ublocks, lblocks, relay, passed,
    uload, lload, near_send, near_recv, far_send, far_recv, pair_send, pair_recv,
    low_send, low_recv, hop_send, hop_recv, pass_recv, goal_send, goal_recv,
):
    r, c = lax.axis_index("row"), lax.axis_index("col")
    core, x = r % 2, c % X
    even = core == 0
    rows = TILE
    chunks = upper.shape[0] // rows
    held = lower.shape[0]
    quarter = held // PARTS

    def dev(dr, dc):
        return (lax.rem(r + dr + n_row, n_row), lax.rem(c + dc + n_col, n_col))

    first = x == 0
    last = x == X - 1
    origin_c = c - x
    goal = (r, origin_c + X - 1)

    barrier = pltpu.get_barrier_semaphore()

    def greet(device):
        pl.semaphore_signal(barrier, inc=1, device_id=device, device_id_type=MESH)

    greet(dev(2, 0))
    greet(dev(jnp.where(even, 1, 3), 0))
    greet(dev(jnp.where(even, 1, -1), 0))

    @pl.when(jnp.logical_not(last))
    def _():
        greet(dev(0, 1))

    @pl.when(last)
    def _():
        for j in range(PARTS - 1):
            greet((r, origin_c + j))

    greet(dev(0, X))

    @pl.when(jnp.logical_not(first))
    def _():
        greet((r, origin_c))

    tile_loads = (
        pltpu.make_async_copy(lower_tiles_in, lower_tiles, tile_load.at[0]),
        pltpu.make_async_copy(upper_tiles_in, upper_tiles, tile_load.at[1]),
    )
    for load in tile_loads:
        load.start()
    def load_upper(i):
        part = pl.ds(pl.multiple_of(i * rows, rows), rows)
        return pltpu.make_async_copy(upper.at[part], ublocks.at[0, part], uload.at[i])

    def load_lower(j):
        part = pl.ds(j * quarter, quarter)
        return pltpu.make_async_copy(lower.at[part], lblocks.at[part], lload.at[j])

    for i in range(BEGIN):
        load_upper(i).start()
    for j in ORDER:
        load_lower(j).start()
    for i in range(BEGIN, chunks):
        load_upper(i).start()

    def near(i):
        part = pl.ds(pl.multiple_of(i * rows, rows), rows)
        return pltpu.make_async_remote_copy(
            ublocks.at[0, part], ublocks.at[2, part], near_send.at[i], near_recv.at[i],
            device_id=dev(-2, 0), device_id_type=MESH,
        )

    far_rows = upper.shape[0] // FARS

    def far(i):
        part = pl.ds(pl.multiple_of(i * far_rows, far_rows), far_rows)
        return pltpu.make_async_remote_copy(
            ublocks.at[0, part], ublocks.at[jnp.where(even, 3, 1), part], far_send.at[i], far_recv.at[i],
            device_id=dev(jnp.where(even, -3, -1), 0), device_id_type=MESH,
        )

    def pair(i):
        part = pl.ds(pl.multiple_of(i * rows, rows), rows)
        return pltpu.make_async_remote_copy(
            ublocks.at[2, part], ublocks.at[jnp.where(even, 1, 3), part], pair_send.at[i], pair_recv.at[i],
            device_id=dev(jnp.where(even, 1, -1), 0), device_id_type=MESH,
        )

    def low():
        return pltpu.make_async_remote_copy(
            lblocks.at[pl.ds(0, held)], lblocks.at[pl.ds(held, held)], low_send, low_recv,
            device_id=dev(0, -1), device_id_type=MESH,
        )

    piece = quarter // PIECES

    def hop(j, h):
        return pltpu.make_async_remote_copy(
            lblocks.at[pl.ds(j * quarter + h * piece, piece)], relay.at[pl.ds(h * piece, piece)],
            hop_send.at[j, h], hop_recv.at[h],
            device_id=(r, lax.rem(origin_c + j, n_col)), device_id_type=MESH,
        )

    def passing(source, target, sem, h):
        return pltpu.make_async_remote_copy(
            source.at[pl.ds(h * piece, piece)], target.at[pl.ds(h * piece, piece)],
            hop_send.at[0, h], sem.at[h], device_id=dev(0, -X), device_id_type=MESH,
        )

    def arrived(j):
        return lblocks.at[pl.ds(pl.multiple_of(held + j * quarter, quarter), quarter)]

    def pass_on(h):
        @pl.when(first)
        def _():
            passing(lblocks.at[pl.ds(0, quarter)], passed, pass_recv, h).start()

        @pl.when(jnp.logical_not(jnp.logical_or(first, last)))
        def _():
            passing(relay, passed, pass_recv, h).start()

        @pl.when(last)
        def _():
            passing(relay, arrived(PARTS - 1), goal_recv.at[PARTS - 1], h).start()

    def to_goal(j, h):
        return pltpu.make_async_remote_copy(
            passed.at[pl.ds(h * piece, piece)], arrived(j).at[pl.ds(h * piece, piece)],
            goal_send.at[h], goal_recv.at[j, h], device_id=goal, device_id_type=MESH,
        )

    def mask_upper(i):
        part = pl.ds(pl.multiple_of(i * rows, rows), rows)
        for k in range(upper.shape[1] // TILE):
            at = (0, part, pl.ds(k * TILE, TILE))
            keep = upper_tiles[i, k].astype(jnp.float32)
            ublocks[at] = ublocks[at] * jnp.full((rows, TILE), keep, jnp.float32).astype(jnp.bfloat16)

    def mask_lower(i):
        part = pl.ds(pl.multiple_of(i * TILE, TILE), TILE)
        for k in range(lower.shape[1] // TILE):
            at = (part, pl.ds(k * TILE, TILE))
            keep = lower_tiles[k, i].astype(jnp.float32)
            lblocks[at] = lblocks[at] * jnp.full((TILE, TILE), keep, jnp.float32).astype(jnp.bfloat16)

    for load in tile_loads:
        load.wait()

    @pl.loop(0, BEGIN)
    def _(i):
        load_upper(i).wait()
        mask_upper(i)

    for j in ORDER:
        load_lower(j).wait()

        @pl.loop(0, quarter // TILE)
        def _(h):
            mask_lower(j * (quarter // TILE) + h)

    pl.semaphore_wait(barrier, 4 + jnp.where(first, 3, 1) + jnp.where(last, 0, 1))

    @pl.loop(0, BEGIN)
    def _(i):
        near(i).start()

    @pl.when(first)
    def _():
        for j in range(1, PARTS):
            for h in range(PIECES):
                hop(j, h).start()

    @pl.when(jnp.logical_not(first))
    def _():
        low().start()

    @pl.loop(BEGIN, chunks)
    def _(i):
        load_upper(i).wait()
        mask_upper(i)

        @pl.when((i + 1) % (chunks // FARS) == 0)
        def _():
            far(i // (chunks // FARS)).start()

    for h in range(PIECES):
        @pl.when(jnp.logical_not(first))
        def _():
            hop(1, h).wait_recv()

        pass_on(h)

    @pl.loop(BEGIN, chunks)
    def _(i):
        near(i).start()

    @pl.when(jnp.logical_not(last))
    def _():
        for h in range(PIECES):
            passing(relay, passed, pass_recv, h).wait_recv()
            to_goal(x, h).start()

    def multiply(i):
        part = pl.ds(pl.multiple_of(i * rows, rows), rows)
        block = ublocks.shape[2]
        total = jnp.zeros((rows, lower.shape[1]), jnp.float32)
        for s in range(STEPS):
            total += jnp.dot(
                ublocks[s, part], lblocks[pl.ds(s * block, block)], preferred_element_type=jnp.float32
            )
        out[part] = total.astype(jnp.bfloat16)

    def step(i):
        near(i).wait_recv()
        pair(i).start()

    def finish(i):
        pair(i).wait_recv()

        @pl.when(i % (chunks // FARS) == 0)
        def _():
            far(i // (chunks // FARS)).wait_recv()

        multiply(i)

    late = chunks - LATE

    @pl.loop(0, late)
    def _(i):
        step(i)

    @pl.when(jnp.logical_not(last))
    def _():
        low().wait_recv()

    @pl.when(last)
    def _():
        for j in range(PARTS):
            for h in range(PIECES):
                to_goal(j, h).wait_recv()

    @pl.loop(0, late - 1)
    def _(i):
        finish(i)

    @pl.loop(late, chunks)
    def _(i):
        finish(i - 1)
        step(i)

    @pl.loop(0, chunks - 1)
    def _(i):
        near(i).wait_send()
        pair(i).wait_send()

    for i in range(FARS):
        far(i).wait_send()

    @pl.when(first)
    def _():
        for h in range(PIECES):
            for j in range(1, PARTS):
                hop(j, h).wait_send()

    @pl.when(jnp.logical_not(first))
    def _():
        low().wait_send()

    for h in range(PIECES):
        passing(relay, passed, pass_recv, h).wait_send()

    @pl.when(jnp.logical_not(last))
    def _():
        for h in range(PIECES):
            to_goal(x, h).wait_send()

    finish(chunks - 1)
    near(chunks - 1).wait_send()
    pair(chunks - 1).wait_send()


def body(upper, lower, upper_tiles, lower_tiles):
    n_row, n_col = lax.axis_size("row"), lax.axis_size("col")
    rows, block = upper.shape
    held, cols = lower.shape
    chunks = rows // TILE
    dma = pltpu.SemaphoreType.DMA

    def run(*refs):
        kernel(n_row, n_col, *refs)

    return pl.pallas_call(
        run,
        out_shape=pltpu.VMEM((rows, cols), jnp.bfloat16),
        in_specs=[pl.BlockSpec(memory_space=pltpu.HBM)] * 4,
        out_specs=pl.BlockSpec(memory_space=pltpu.VMEM),
        scratch_shapes=[
            pltpu.SMEM(upper_tiles.shape, jnp.int32),
            pltpu.SMEM(lower_tiles.shape[::-1], jnp.int32),
            dma((2,)),
            pltpu.VMEM((STEPS, rows, block), jnp.bfloat16),
            pltpu.VMEM((2 * held, cols), jnp.bfloat16),
            pltpu.VMEM((held // PARTS, cols), jnp.bfloat16),
            pltpu.VMEM((held // PARTS, cols), jnp.bfloat16),
            dma((chunks,)), dma((PARTS,)),
            dma((chunks,)), dma((chunks,)),
            dma((FARS,)), dma((FARS,)),
            dma((chunks,)), dma((chunks,)),
            dma, dma,
            dma((PARTS, PIECES)), dma((PIECES,)), dma((PIECES,)), dma((PIECES,)), dma((PARTS, PIECES)),
        ],
        compiler_params=pltpu.CompilerParams(
            collective_id=0, has_side_effects=True, vmem_limit_bytes=40 * 1024 * 1024
        ),
        cost_estimate=pl.CostEstimate(
            flops=2 * STEPS * rows * block * cols,
            bytes_accessed=2 * (rows * block + held * cols + rows * cols),
            transcendentals=0,
        ),
        name="corner_product",
    )(*(pltpu.with_memory_space_constraint(a, pltpu.HBM) for a in (upper_tiles, lower_tiles.T, upper, lower)))


def solution(mesh):
    spec = P("col", "row")
    return jax.shard_map(body, mesh=mesh, in_specs=(spec,) * 4, out_specs=spec, check_vma=False)
```

```python
import jax
import jax.numpy as jnp
from jax import lax
from jax.experimental import pallas as pl
from jax.experimental.pallas import tpu as pltpu
from jax.sharding import PartitionSpec as P

STEPS = 4
TILE = 128
X = 4
BEGIN = 3
LATE = 3
FARS = 1
PIECES = 1
ORDER = (1, 2, 3, 0)
PARTS = 4
MESH = pl.DeviceIdType.MESH


def kernel(
    n_row, n_col, upper_tiles_in, lower_tiles_in, upper, lower, out,
    upper_tiles, lower_tiles, tile_load, ublocks, lblocks, relay, passed,
    uload, lload, near_send, near_recv, far_send, far_recv, pair_send, pair_recv,
    low_send, low_recv, hop_send, hop_recv, pass_recv, goal_send, goal_recv,
):
    r, c = lax.axis_index("row"), lax.axis_index("col")
    core, x = r % 2, c % X
    even = core == 0
    rows = TILE
    chunks = upper.shape[0] // rows
    held = lower.shape[0]
    quarter = held // PARTS

    def dev(dr, dc):
        return (lax.rem(r + dr + n_row, n_row), lax.rem(c + dc + n_col, n_col))

    first = x == 0
    last = x == X - 1
    origin_c = c - x
    goal = (r, origin_c + X - 1)

    barrier = pltpu.get_barrier_semaphore()

    def greet(device):
        pl.semaphore_signal(barrier, inc=1, device_id=device, device_id_type=MESH)

    greet(dev(2, 0))
    greet(dev(jnp.where(even, 1, 3), 0))
    greet(dev(jnp.where(even, 1, -1), 0))

    @pl.when(jnp.logical_not(last))
    def _():
        greet(dev(0, 1))

    @pl.when(last)
    def _():
        for j in range(PARTS - 1):
            greet((r, origin_c + j))

    greet(dev(0, X))

    @pl.when(jnp.logical_not(first))
    def _():
        greet((r, origin_c))

    tile_loads = (
        pltpu.make_async_copy(lower_tiles_in, lower_tiles, tile_load.at[0]),
        pltpu.make_async_copy(upper_tiles_in, upper_tiles, tile_load.at[1]),
    )
    for load in tile_loads:
        load.start()
    def load_upper(i):
        part = pl.ds(pl.multiple_of(i * rows, rows), rows)
        return pltpu.make_async_copy(upper.at[part], ublocks.at[0, part], uload.at[i])

    def load_lower(j):
        part = pl.ds(j * quarter, quarter)
        return pltpu.make_async_copy(lower.at[part], lblocks.at[part], lload.at[j])

    for i in range(BEGIN):
        load_upper(i).start()
    for j in ORDER:
        load_lower(j).start()
    for i in range(BEGIN, chunks):
        load_upper(i).start()

    def near(i):
        part = pl.ds(pl.multiple_of(i * rows, rows), rows)
        return pltpu.make_async_remote_copy(
            ublocks.at[0, part], ublocks.at[2, part], near_send.at[i], near_recv.at[i],
            device_id=dev(-2, 0), device_id_type=MESH,
        )

    far_rows = upper.shape[0] // FARS

    def far(i):
        part = pl.ds(pl.multiple_of(i * far_rows, far_rows), far_rows)
        return pltpu.make_async_remote_copy(
            ublocks.at[0, part], ublocks.at[jnp.where(even, 3, 1), part], far_send.at[i], far_recv.at[i],
            device_id=dev(jnp.where(even, -3, -1), 0), device_id_type=MESH,
        )

    def pair(i):
        part = pl.ds(pl.multiple_of(i * rows, rows), rows)
        return pltpu.make_async_remote_copy(
            ublocks.at[2, part], ublocks.at[jnp.where(even, 1, 3), part], pair_send.at[i], pair_recv.at[i],
            device_id=dev(jnp.where(even, 1, -1), 0), device_id_type=MESH,
        )

    def low():
        return pltpu.make_async_remote_copy(
            lblocks.at[pl.ds(0, held)], lblocks.at[pl.ds(held, held)], low_send, low_recv,
            device_id=dev(0, -1), device_id_type=MESH,
        )

    piece = quarter // PIECES

    def hop(j, h):
        return pltpu.make_async_remote_copy(
            lblocks.at[pl.ds(j * quarter + h * piece, piece)], relay.at[pl.ds(h * piece, piece)],
            hop_send.at[j, h], hop_recv.at[h],
            device_id=(r, lax.rem(origin_c + j, n_col)), device_id_type=MESH,
        )

    def passing(source, target, sem, h):
        return pltpu.make_async_remote_copy(
            source.at[pl.ds(h * piece, piece)], target.at[pl.ds(h * piece, piece)],
            hop_send.at[0, h], sem.at[h], device_id=dev(0, -X), device_id_type=MESH,
        )

    def arrived(j):
        return lblocks.at[pl.ds(pl.multiple_of(held + j * quarter, quarter), quarter)]

    def pass_on(h):
        @pl.when(first)
        def _():
            passing(lblocks.at[pl.ds(0, quarter)], passed, pass_recv, h).start()

        @pl.when(jnp.logical_not(jnp.logical_or(first, last)))
        def _():
            passing(relay, passed, pass_recv, h).start()

        @pl.when(last)
        def _():
            passing(relay, arrived(PARTS - 1), goal_recv.at[PARTS - 1], h).start()

    def to_goal(j, h):
        return pltpu.make_async_remote_copy(
            passed.at[pl.ds(h * piece, piece)], arrived(j).at[pl.ds(h * piece, piece)],
            goal_send.at[h], goal_recv.at[j, h], device_id=goal, device_id_type=MESH,
        )

    def mask_upper(i):
        part = pl.ds(pl.multiple_of(i * rows, rows), rows)
        for k in range(upper.shape[1] // TILE):
            at = (0, part, pl.ds(k * TILE, TILE))
            keep = upper_tiles[i, k].astype(jnp.float32)
            ublocks[at] = ublocks[at] * jnp.full((rows, TILE), keep, jnp.float32).astype(jnp.bfloat16)

    def mask_lower(i):
        part = pl.ds(pl.multiple_of(i * TILE, TILE), TILE)
        for k in range(lower.shape[1] // TILE):
            at = (part, pl.ds(k * TILE, TILE))
            keep = lower_tiles[k, i].astype(jnp.float32)
            lblocks[at] = lblocks[at] * jnp.full((TILE, TILE), keep, jnp.float32).astype(jnp.bfloat16)

    for load in tile_loads:
        load.wait()

    @pl.loop(0, BEGIN)
    def _(i):
        load_upper(i).wait()
        mask_upper(i)

    for j in ORDER:
        load_lower(j).wait()

        @pl.loop(0, quarter // TILE)
        def _(h):
            mask_lower(j * (quarter // TILE) + h)

    pl.semaphore_wait(barrier, 4 + jnp.where(first, 3, 1) + jnp.where(last, 0, 1))

    @pl.loop(0, BEGIN)
    def _(i):
        near(i).start()

    @pl.when(first)
    def _():
        for j in range(1, PARTS):
            for h in range(PIECES):
                hop(j, h).start()

    @pl.when(jnp.logical_not(first))
    def _():
        low().start()

    @pl.loop(BEGIN, chunks)
    def _(i):
        load_upper(i).wait()
        mask_upper(i)

        @pl.when((i + 1) % (chunks // FARS) == 0)
        def _():
            far(i // (chunks // FARS)).start()

    for h in range(PIECES):
        @pl.when(jnp.logical_not(first))
        def _():
            hop(1, h).wait_recv()

        pass_on(h)

    @pl.loop(BEGIN, chunks)
    def _(i):
        near(i).start()

    @pl.when(jnp.logical_not(last))
    def _():
        for h in range(PIECES):
            passing(relay, passed, pass_recv, h).wait_recv()
            to_goal(x, h).start()

    def multiply(i):
        part = pl.ds(pl.multiple_of(i * rows, rows), rows)
        block = ublocks.shape[2]
        total = jnp.zeros((rows, lower.shape[1]), jnp.float32)
        for s in range(STEPS):
            total += jnp.dot(
                ublocks[s, part], lblocks[pl.ds(s * block, block)], preferred_element_type=jnp.float32
            )
        out[part] = total.astype(jnp.bfloat16)

    def step(i):
        near(i).wait_recv()
        pair(i).start()

    def finish(i):
        pair(i).wait_recv()

        @pl.when(i % (chunks // FARS) == 0)
        def _():
            far(i // (chunks // FARS)).wait_recv()

        multiply(i)

    late = chunks - LATE

    @pl.loop(0, late)
    def _(i):
        step(i)

    @pl.when(jnp.logical_not(last))
    def _():
        low().wait_recv()

    @pl.when(last)
    def _():
        for j in range(PARTS):
            for h in range(PIECES):
                to_goal(j, h).wait_recv()

    @pl.loop(0, late - 1)
    def _(i):
        finish(i)

    @pl.loop(late, chunks)
    def _(i):
        finish(i - 1)
        step(i)

    @pl.loop(0, chunks - 1)
    def _(i):
        near(i).wait_send()
        pair(i).wait_send()

    for i in range(FARS):
        far(i).wait_send()

    @pl.when(first)
    def _():
        for h in range(PIECES):
            for j in range(1, PARTS):
                hop(j, h).wait_send()

    @pl.when(jnp.logical_not(first))
    def _():
        low().wait_send()

    for h in range(PIECES):
        passing(relay, passed, pass_recv, h).wait_send()

    @pl.when(jnp.logical_not(last))
    def _():
        for h in range(PIECES):
            to_goal(x, h).wait_send()

    finish(chunks - 1)
    near(chunks - 1).wait_send()
    pair(chunks - 1).wait_send()


def body(upper, lower, upper_tiles, lower_tiles):
    n_row, n_col = lax.axis_size("row"), lax.axis_size("col")
    rows, block = upper.shape
    held, cols = lower.shape
    chunks = rows // TILE
    dma = pltpu.SemaphoreType.DMA

    def run(*refs):
        kernel(n_row, n_col, *refs)

    return pl.pallas_call(
        run,
        out_shape=pltpu.VMEM((rows, cols), jnp.bfloat16),
        in_specs=[pl.BlockSpec(memory_space=pltpu.HBM)] * 4,
        out_specs=pl.BlockSpec(memory_space=pltpu.VMEM),
        scratch_shapes=[
            pltpu.SMEM(upper_tiles.shape, jnp.int32),
            pltpu.SMEM(lower_tiles.shape[::-1], jnp.int32),
            dma((2,)),
            pltpu.VMEM((STEPS, rows, block), jnp.bfloat16),
            pltpu.VMEM((2 * held, cols), jnp.bfloat16),
            pltpu.VMEM((held // PARTS, cols), jnp.bfloat16),
            pltpu.VMEM((held // PARTS, cols), jnp.bfloat16),
            dma((chunks,)), dma((PARTS,)),
            dma((chunks,)), dma((chunks,)),
            dma((FARS,)), dma((FARS,)),
            dma((chunks,)), dma((chunks,)),
            dma, dma,
            dma((PARTS, PIECES)), dma((PIECES,)), dma((PIECES,)), dma((PIECES,)), dma((PARTS, PIECES)),
        ],
        compiler_params=pltpu.CompilerParams(
            collective_id=0, has_side_effects=True, vmem_limit_bytes=40 * 1024 * 1024
        ),
        cost_estimate=pl.CostEstimate(
            flops=2 * STEPS * rows * block * cols,
            bytes_accessed=2 * (rows * block + held * cols + rows * cols),
            transcendentals=0,
        ),
        name="corner_product",
    )(*(pltpu.with_memory_space_constraint(a, pltpu.HBM) for a in (upper_tiles, lower_tiles.T, upper, lower)))


def solution(mesh):
    spec = P("col", "row")
    return jax.shard_map(body, mesh=mesh, in_specs=(spec,) * 4, out_specs=spec, check_vma=False)
```
